1024 devices in a mesh: half: 2 (over core), dp: 16 (over x, y), tensor: 32 (over z).
Axes of the slice: x: 4, y: 4, z: 32, core: 2. Of those that a mesh axis runs over, the one named last changes fastest.
Arguments:
- history: bfloat16 [16, 128, 512, 1024], P('dp', ('half', 'tensor')), may hold values from -6 to 6
- queries: bfloat16 [16, 128, 64, 1024], P('dp', ('half', 'tensor'))
- lengths: int32 [16, 128], P('dp', ('half', 'tensor')), may hold values from 128 to 512, as said below
- assignment: int32 [16, 128], P('dp'), may hold values from 0 to 127, each once within a row
- key_weight: bfloat16 [1024, 1024], replicated, may hold values from -0.1875 to 0.1875
- key_gain: float32 [1024], replicated, may hold values from 0.5 to 2
- interest_gain: float32 [256], replicated, may hold values from 0.5 to 2
- sparse_embed: bfloat16 [2048, 256, 256], P('dp', ('half', 'tensor')), may hold values from -6 to 6
- proj_interest: bfloat16 [256, 12], P(('half', 'tensor')), may hold values from -0.25 to 0.25
- proj_sparse: bfloat16 [256, 12], P(('half', 'tensor')), may hold values from -0.25 to 0.25
- cot_interest: bfloat16 [2048, 256, 12], P('dp', ('half', 'tensor')), may hold values from -6 to 6
- cot_sparse: bfloat16 [2048, 256, 12], P('dp', ('half', 'tensor')), may hold values from -6 to 6
Outputs:
- grad_interest: bfloat16 [2048, 256, 256], P('dp', ('half', 'tensor'))
- grad_sparse: bfloat16 [2048, 256, 256], P('dp', ('half', 'tensor'))
- grad_proj_interest: float32 [256, 12], P(('half', 'tensor'))
- grad_proj_sparse: float32 [256, 12], P(('half', 'tensor'))
The draws below stay inside these ranges and needn't reach their ends.
Inputs may be any that keep to these rules, and one draw needn't show every extreme that they name: `lengths`: every length is a multiple of 128; in every batch shard some user has exactly 512.
All inputs are finite; a program needn't handle non-finite values.
Results may differ from the reference program's by a relative error of at most 0.0085.
Values may be sent and summed in bfloat16 or wider, within the bound.
No kernel may reach another device: no remote copies, remote signals or barrier semaphores. Data moves between devices by JAX's collectives and lax.ppermute only.
A program may use at most 32 MiB of HBM per device.

```python
import math
import jax
import jax.numpy as jnp
from jax import lax

D = 1024
HEADS = 8
EMB = 256
QUERIES = 64
SPARSE = 256
FM_RANK = 12
BLOCK = 128
LEN = 512
INTEREST = 256
GROUP_USERS = 128
BATCH = 2048
N_DP = 16


def draw_queries(key, part):
    key = jax.random.fold_in(key, 11)
    shape_all = (N_DP, GROUP_USERS, QUERIES, D)
    normal_part = jax.random.truncated_normal(jax.random.fold_in(key, 1), -6.0, 6.0, shape_all, jnp.float32)
    return normal_part.astype(jnp.bfloat16)


def draw_lengths(key, part):
    key = jax.random.fold_in(key, 23)
    block_total = LEN // BLOCK
    blocks_drawn = jax.random.randint(jax.random.fold_in(key, 1), (N_DP, GROUP_USERS), 1, block_total + 1)
    longest = jax.random.randint(jax.random.fold_in(key, 2), (N_DP, 1), 0, GROUP_USERS)
    positions = jnp.arange(GROUP_USERS).astype(jnp.int32)[None, :]
    blocks_drawn = jnp.where(positions == longest, block_total, blocks_drawn)
    return (blocks_drawn * BLOCK).astype(jnp.int32)


def levels(key, extent, cuts, smallest, largest):
    level = 1.0
    for dim, parts in cuts:
        draws = jax.random.uniform(jax.random.fold_in(jax.random.fold_in(key, 6), dim), (parts,), jnp.float32, smallest / len(cuts), largest / len(cuts))
        level = level * jnp.repeat(jnp.exp(draws), extent[dim] // parts).reshape((-1,) + (1,) * (len(extent) - 1 - dim))
    return level


def scatter_about(own_key, extent, width, bound, shards=(), kind=jnp.bfloat16):
    values = jax.random.normal(own_key, extent, jnp.float32) * width
    if len(shards) > 0:
        values = levels(own_key, extent, shards, -0.22, 0.18) * values
    return jnp.clip(values, min=-bound, max=bound).astype(kind)


def setup_inputs(seed: int = 0) -> dict:
    keys = jax.random.split(jax.random.key(seed), 13)
    return {
        "history": scatter_about(keys[0], (N_DP, GROUP_USERS, LEN, D), 1.0, 6.0, ((0, 16), (1, 64))),
        "queries": draw_queries(jax.random.fold_in(keys[12], 71), 0),
        "lengths": draw_lengths(jax.random.fold_in(keys[12], 71), 0),
        "assignment": jax.vmap(lambda own: jax.random.permutation(own, GROUP_USERS))(jax.random.split(keys[3], N_DP)).reshape((N_DP, GROUP_USERS)).astype(jnp.int32),
        "key_weight": scatter_about(keys[4], (D, D), D ** -0.5, 0.1875),
        "key_gain": jnp.clip(jnp.exp(jax.random.uniform(keys[5], (D,), jnp.float32, math.log(0.5), math.log(2.0))), 0.5, 2.0),
        "interest_gain": jnp.clip(jnp.exp(jax.random.uniform(keys[6], (EMB,), jnp.float32, math.log(0.5), math.log(2.0))), 0.5, 2.0),
        "sparse_embed": scatter_about(keys[7], (BATCH, SPARSE, EMB), 1.0, 6.0, ((0, 16), (1, 64))),
        "proj_interest": scatter_about(keys[8], (INTEREST, FM_RANK), (INTEREST + SPARSE) ** -0.5, 0.25, ((0, 64),)),
        "proj_sparse": scatter_about(keys[9], (SPARSE, FM_RANK), (INTEREST + SPARSE) ** -0.5, 0.25, ((0, 64),)),
        "cot_interest": scatter_about(keys[10], (BATCH, INTEREST, FM_RANK), 1.0, 6.0, ((0, 16), (1, 64))),
        "cot_sparse": scatter_about(keys[11], (BATCH, SPARSE, FM_RANK), 1.0, 6.0, ((0, 16), (1, 64))),
    }


def encode_user(history_rows, user_query, user_length, key_weight, key_gain, interest_gain):
    head_dim = D // HEADS
    raw_keys = jnp.dot(history_rows, key_weight, preferred_element_type=jnp.float32)
    by_head = raw_keys.reshape(LEN, HEADS, head_dim)
    shrink = lax.rsqrt(lax.optimization_barrier(jnp.mean(by_head * by_head, axis=-1, keepdims=True)) + 1e-06)
    key_block = ((by_head * shrink).reshape(LEN, D) * key_gain.astype(jnp.float32)).astype(jnp.bfloat16)
    query_f = user_query.astype(jnp.float32).reshape(QUERIES, HEADS, head_dim)
    key_f = key_block.astype(jnp.float32).reshape(LEN, HEADS, head_dim)
    scores = jnp.einsum('qhd,lhd->hql', query_f, key_f) / math.sqrt(head_dim)
    live_mask = jnp.arange(LEN).astype(jnp.int32) < user_length
    scores = jnp.where(live_mask[None, None, :], scores, -1e+30)
    row_max = lax.optimization_barrier(jnp.max(scores, axis=-1, keepdims=True))
    expo = jnp.exp(scores - row_max)
    attention = (expo / lax.optimization_barrier(jnp.sum(expo, axis=-1, keepdims=True))).astype(jnp.bfloat16)
    values_f = history_rows.astype(jnp.float32).reshape(LEN, HEADS, head_dim)
    pooled = jnp.einsum('hql,lhd->qhd', attention.astype(jnp.float32), values_f)
    pieces = pooled.reshape(QUERIES, D // EMB, EMB)
    norm_inv = lax.rsqrt(lax.optimization_barrier(jnp.mean(pieces * pieces, axis=-1, keepdims=True)) + 1e-06)
    normed = pieces * norm_inv * interest_gain.astype(jnp.float32)
    return normed.reshape(INTEREST, EMB).astype(jnp.bfloat16)

def place_rows(pooled_shard, batch_rows):
    return jnp.zeros_like(pooled_shard).at[batch_rows].set(pooled_shard)

def reference(history, queries, lengths, assignment, key_weight, key_gain, interest_gain, sparse_embed, proj_interest, proj_sparse, cot_interest, cot_sparse):
    flat_history = history.reshape(N_DP * GROUP_USERS, LEN, D)
    flat_queries = queries.reshape(N_DP * GROUP_USERS, QUERIES, D)
    flat_lengths = lengths.reshape(N_DP * GROUP_USERS)

    def one_user(packed):
        return encode_user(packed[0], packed[1], packed[2], key_weight, key_gain, interest_gain)
    local_interest = lax.map(one_user, (flat_history, flat_queries, flat_lengths))
    local_interest = local_interest.reshape(N_DP, GROUP_USERS, INTEREST, EMB)
    interest = jax.vmap(place_rows)(local_interest, assignment).reshape(BATCH, INTEREST, EMB)
    factor = 1.0 / math.sqrt(EMB)
    inter_f = interest.astype(jnp.float32)
    sparse_f = sparse_embed.astype(jnp.float32)
    proj_i = proj_interest.astype(jnp.float32)
    proj_s = proj_sparse.astype(jnp.float32)
    cot_i = cot_interest.astype(jnp.float32)
    cot_s = cot_sparse.astype(jnp.float32)
    fm_state = jnp.einsum('bne,nk->bke', inter_f, proj_i) + jnp.einsum('bne,nk->bke', sparse_f, proj_s)
    state_round = fm_state.astype(jnp.bfloat16).astype(jnp.float32)
    state_grad = (jnp.einsum('bne,bnk->bke', inter_f, cot_i) + jnp.einsum('bne,bnk->bke', sparse_f, cot_s)) * factor
    grad_round = state_grad.astype(jnp.bfloat16).astype(jnp.float32)
    grad_interest = (jnp.einsum('bnk,bke->bne', cot_i, state_round) * factor + jnp.einsum('nk,bke->bne', proj_i, grad_round)).astype(jnp.bfloat16)
    grad_sparse = (jnp.einsum('bnk,bke->bne', cot_s, state_round) * factor + jnp.einsum('nk,bke->bne', proj_s, grad_round)).astype(jnp.bfloat16)
    grad_proj_interest = jnp.einsum('bne,bke->nk', inter_f, grad_round) / BATCH
    grad_proj_sparse = jnp.einsum('bne,bke->nk', sparse_f, grad_round) / BATCH
    return (grad_interest, grad_sparse, grad_proj_interest, grad_proj_sparse)
```

```python
import functools
import math

import jax
import jax.numpy as jnp
from jax import lax
from jax.experimental import pallas as pl
from jax.experimental.pallas import tpu as pltpu
from jax.sharding import PartitionSpec as P

HEADS = 8
EMB = 256
RANK = 12
STATE = 2 * RANK
SIDE = 2 * EMB
PACKED = 2 * EMB + 128
NEAR = 4
ALL = ("half", "tensor")
F32 = jnp.float32
BF16 = jnp.bfloat16


def key_rows(history_rows, key_weight, key_gain):
    raw_keys = jnp.dot(history_rows, key_weight, preferred_element_type=F32)
    row_count, model_width = raw_keys.shape
    by_head = raw_keys.reshape(row_count, HEADS, model_width // HEADS)
    shrink = lax.rsqrt(jnp.mean(by_head * by_head, axis=-1, keepdims=True) + 1e-06)
    return ((by_head * shrink).reshape(row_count, model_width) * key_gain).astype(BF16)


def encode_user(history_rows, user_query, user_length, key_weight, key_gain, interest_gain):
    seq_len, model_width = history_rows.shape
    head_dim = model_width // HEADS
    key_block = key_rows(history_rows, key_weight, key_gain)
    query_heads = user_query.reshape(user_query.shape[0], HEADS, head_dim)
    key_heads = key_block.reshape(seq_len, HEADS, head_dim)
    scores = jnp.einsum(
        "qhd,lhd->hql", query_heads, key_heads, preferred_element_type=F32
    ) / math.sqrt(head_dim)
    live_mask = lax.broadcasted_iota(jnp.int32, (1, 1, seq_len), 2) < user_length
    scores = jnp.where(live_mask, scores, -1e30)
    row_max = jnp.max(scores, axis=-1, keepdims=True)
    expo = jnp.exp(scores - row_max)
    attention = (expo / jnp.sum(expo, axis=-1, keepdims=True)).astype(BF16)
    value_heads = history_rows.reshape(seq_len, HEADS, head_dim)
    pooled = jnp.einsum("hql,lhd->qhd", attention, value_heads, preferred_element_type=F32)
    pieces = pooled.reshape(user_query.shape[0], model_width // EMB, EMB)
    norm_inv = lax.rsqrt(jnp.mean(pieces * pieces, axis=-1, keepdims=True) + 1e-06)
    normed = pieces * norm_inv * interest_gain
    return normed.reshape(user_query.shape[0] * (model_width // EMB), EMB).astype(BF16)


def pack_kernel(rows_ref, by_slot_ref, sparse_ref, cot_ref, proj_ref, out_ref):
    devices, width = out_ref.shape[0], sparse_ref.shape[1]
    batch = sparse_ref.shape[0]
    for user in range(2 * devices):
        lanes = slice((user % 2) * EMB, (user % 2 + 1) * EMB)
        out_ref[user // 2, :, lanes] = sparse_ref[rows_ref[user]]
    picks = []
    for slot in range(2):
        wanted = by_slot_ref[slot : slot + 1, :]
        row_of = lax.broadcasted_iota(jnp.int32, (batch, devices), 0)
        picks.append((row_of == wanted).astype(BF16))
    for j in range(width):
        parts = [
            lax.dot_general(
                pick, cot_ref[j], (((0,), (1,)), ((), ())), preferred_element_type=F32
            )
            for pick in picks
        ]
        parts.append(jnp.broadcast_to(proj_ref[j : j + 1, :], (devices, STATE)))
        parts.append(jnp.zeros((devices, 128 - 3 * STATE), F32))
        out_ref[:, j, SIDE:] = jnp.concatenate(parts, axis=1).astype(BF16)


def pack(rows, by_slot, sparse_embed, cots, projs):
    devices = by_slot.shape[1]
    width = sparse_embed.shape[1]
    vmem = pl.BlockSpec(memory_space=pltpu.VMEM)
    return pl.pallas_call(
        pack_kernel,
        out_shape=jax.ShapeDtypeStruct((devices, width, PACKED), BF16),
        in_specs=[pl.BlockSpec(memory_space=pltpu.SMEM), vmem, vmem, vmem, vmem],
        out_specs=vmem,
        compiler_params=pltpu.CompilerParams(vmem_limit_bytes=32 * 2**20),
        name="pack_rows",
    )(rows, by_slot, sparse_embed, cots, projs)


def state_kernel(factor, packed_ref, interest_ref, state_ref, part_ref, scratch):
    contract_rows = (((0,), (0,)), ((), ()))
    contract_lanes = (((1,), (1,)), ((), ()))
    side = packed_ref[:, SIDE:]
    proj = side[:, 2 * STATE : 3 * STATE]
    total_int, total_spa = None, None
    for slot in range(2):
        interest = interest_ref[slot]
        sparse = packed_ref[:, slot * EMB : (slot + 1) * EMB]
        cot = side[:, slot * STATE : (slot + 1) * STATE]
        left_int = jnp.concatenate([proj[:, :RANK], cot[:, :RANK]], axis=1)
        left_spa = jnp.concatenate([proj[:, RANK:], cot[:, RANK:]], axis=1)
        summed = lax.dot_general(
            left_int, interest, contract_rows, preferred_element_type=F32
        ) + lax.dot_general(left_spa, sparse, contract_rows, preferred_element_type=F32)
        is_state = lax.broadcasted_iota(jnp.int32, summed.shape, 0) < RANK
        rounded = jnp.where(is_state, summed, summed * factor).astype(BF16)
        state_ref[slot * STATE : (slot + 1) * STATE, :] = rounded
        grad = rounded[RANK:, :]
        part_int = lax.dot_general(interest, grad, contract_lanes, preferred_element_type=F32)
        part_spa = lax.dot_general(sparse, grad, contract_lanes, preferred_element_type=F32)
        total_int = part_int if total_int is None else total_int + part_int
        total_spa = part_spa if total_spa is None else total_spa + part_spa
    rows = total_int.shape[0]
    scratch[...] = jnp.concatenate(
        [total_int, total_spa, jnp.zeros((rows, 128 - STATE), F32)], axis=1
    )
    width = rows // part_ref.shape[0]
    merged = scratch[pl.ds(0, part_ref.shape[0], stride=width), :]
    for j in range(1, width):
        piece = scratch[pl.ds(j, part_ref.shape[0], stride=width), :]
        merged = merged + pltpu.roll(piece, j * STATE, 1)
    part_ref[...] = merged


def make_state(packed, interest, devices):
    vmem = pl.BlockSpec(memory_space=pltpu.VMEM)
    rows = packed.shape[0]
    return pl.pallas_call(
        functools.partial(state_kernel, 1.0 / math.sqrt(EMB)),
        out_shape=(
            jax.ShapeDtypeStruct((2 * STATE, EMB), BF16),
            jax.ShapeDtypeStruct((devices, 128), F32),
        ),
        in_specs=[vmem, vmem],
        out_specs=(vmem, vmem),
        scratch_shapes=[pltpu.VMEM((rows, 128), F32)],
        compiler_params=pltpu.CompilerParams(vmem_limit_bytes=32 * 2**20),
        name="make_state",
    )(packed, interest)


def embed_kernel(rows_ref, left_int_ref, left_spa_ref, own_ref, other_ref, int_ref, spa_ref):
    blocks = left_int_ref.shape[0]
    for block in range(blocks):
        source = own_ref if block < blocks // 2 else other_ref
        first = (block % (blocks // 2)) * NEAR
        states = source[first : first + NEAR].reshape(NEAR * 2 * STATE, EMB)
        got_int = jnp.dot(left_int_ref[block], states, preferred_element_type=F32)
        got_spa = jnp.dot(left_spa_ref[block], states, preferred_element_type=F32)
        for i in range(2 * NEAR):
            row = rows_ref[block * 2 * NEAR + i]
            int_ref[row] = got_int[8 * i : 8 * i + 4, :].astype(BF16)
            spa_ref[row] = got_spa[8 * i : 8 * i + 4, :].astype(BF16)


def embed_grads(rows, left_int, left_spa, own, other, width):
    vmem = pl.BlockSpec(memory_space=pltpu.VMEM)
    out = jax.ShapeDtypeStruct((rows.shape[0], width, EMB), BF16)
    return pl.pallas_call(
        embed_kernel,
        out_shape=(out, out),
        in_specs=[pl.BlockSpec(memory_space=pltpu.SMEM), vmem, vmem, vmem, vmem],
        out_specs=(vmem, vmem),
        compiler_params=pltpu.CompilerParams(vmem_limit_bytes=32 * 2**20),
        name="embed_grads",
    )(rows, left_int, left_spa, own, other)


def left_blocks(cot_rows, proj, factor):
    users, width, rank = cot_rows.shape
    rows = jnp.concatenate(
        [cot_rows * factor, jnp.broadcast_to(proj[None], (users, width, rank))], axis=-1
    ).astype(BF16)
    rows = jnp.pad(rows, ((0, 0), (0, 8 - width), (0, 0)))
    per_block = 2 * NEAR
    rows = rows.reshape(users // per_block, per_block, 8, 1, 2 * rank)
    eye = jnp.eye(per_block, dtype=BF16).reshape(1, per_block, 1, per_block, 1)
    return (rows * eye).reshape(users // per_block, per_block * 8, per_block * 2 * rank)


def on_device(
    history,
    queries,
    lengths,
    assignment,
    key_weight,
    key_gain,
    interest_gain,
    sparse_embed,
    proj_interest,
    proj_sparse,
    cot_interest,
    cot_sparse,
):
    batch_rows = assignment[0]
    batch_local, width, _ = sparse_embed.shape
    devices = batch_local // 2
    tensor = lax.axis_size("tensor")
    halves = lax.axis_size("half")
    factor = 1.0 / math.sqrt(EMB)

    by_slot = batch_rows.reshape(devices, 2).T
    cots = jnp.concatenate([cot_interest, cot_sparse], axis=-1).transpose(1, 2, 0)
    projs = jnp.concatenate([proj_interest, proj_sparse], axis=-1).astype(F32)
    packed = pack(batch_rows, by_slot, sparse_embed, cots, projs)
    arrived = lax.all_to_all(packed, ALL, split_axis=0, concat_axis=0, tiled=True)

    user_count = history.shape[1]
    encoded = [
        encode_user(
            history[0, user_slot],
            queries[0, user_slot],
            lengths[0, user_slot],
            key_weight,
            key_gain,
            interest_gain,
        )
        for user_slot in range(user_count)
    ]
    interest = jnp.stack(encoded, axis=0)

    folded = [0, 2, 3, 1]
    far_count = tensor // NEAR
    far_groups = [[i + NEAR * m for m in range(far_count)] for i in range(NEAR)]
    near_groups = [[NEAR * i + j for j in folded] for i in range(far_count)]
    order = [f + NEAR * m for f in folded for m in range(far_count)]
    my_half = lax.axis_index("half")
    tables = batch_rows.reshape(halves, tensor, 2)
    tables = tables[:, jnp.array(order), :]
    tables = jnp.where(my_half == 0, tables, tables[::-1])
    ordered_rows = tables.reshape(batch_local)
    selector = (
        ordered_rows[:, None] == lax.broadcasted_iota(jnp.int32, (batch_local, batch_local), 1)
    ).astype(BF16)
    ordered_cots = jnp.einsum("ub,jkb->ujk", selector, cots, preferred_element_type=F32)
    left_int = left_blocks(ordered_cots[:, :, :RANK], proj_interest.astype(F32), factor)
    left_spa = left_blocks(ordered_cots[:, :, RANK:], proj_sparse.astype(F32), factor)

    state, part = make_state(arrived.reshape(devices * width, PACKED), interest, devices)

    far = lax.all_gather(state, "tensor", axis=0, tiled=False, axis_index_groups=far_groups)
    own = lax.all_gather(far, "tensor", axis=0, tiled=True, axis_index_groups=near_groups)
    other = lax.ppermute(own, "half", [(i, (i + 1) % halves) for i in range(halves)])

    parts = lax.all_to_all(part, ALL, split_axis=0, concat_axis=0, tiled=True)
    mine = jnp.sum(parts, axis=0)
    shards = lax.axis_size("dp")
    spread = jnp.broadcast_to(mine[None], (shards, mine.shape[0]))
    shares = lax.all_to_all(spread, "dp", split_axis=0, concat_axis=0, tiled=True)
    batch_total = shards * batch_local
    proj_grads = jnp.sum(shares, axis=0)[: width * STATE].reshape(width, STATE) / batch_total

    grad_interest, grad_sparse = embed_grads(ordered_rows, left_int, left_spa, own, other, width)
    return (grad_interest, grad_sparse, proj_grads[:, :RANK], proj_grads[:, RANK:])


def solution(mesh):
    placed = (
        P("dp", ("half", "tensor"), None, None),
        P("dp", ("half", "tensor"), None, None),
        P("dp", ("half", "tensor")),
        P("dp", None),
        P(),
        P(),
        P(),
        P("dp", ("half", "tensor"), None),
        P(("half", "tensor"), None),
        P(("half", "tensor"), None),
        P("dp", ("half", "tensor"), None),
        P("dp", ("half", "tensor"), None),
    )
    return jax.shard_map(
        on_device,
        mesh=mesh,
        in_specs=placed,
        out_specs=(
            P("dp", ("half", "tensor"), None),
            P("dp", ("half", "tensor"), None),
            P(("half", "tensor"), None),
            P(("half", "tensor"), None),
        ),
        check_vma=False,
    )
```

```python
import functools
import math

import jax
import jax.numpy as jnp
from jax import lax
from jax.experimental import pallas as pl
from jax.experimental.pallas import tpu as pltpu
from jax.sharding import PartitionSpec as P

HEADS = 8
EMB = 256
RANK = 12
STATE = 2 * RANK
SIDE = 2 * EMB
PACKED = 2 * EMB + 128
NEAR = 4
PAIR = 2
ALL = ("half", "tensor")
F32 = jnp.float32
BF16 = jnp.bfloat16


def key_rows(history_rows, key_weight, key_gain):
    raw_keys = jnp.dot(history_rows, key_weight, preferred_element_type=F32)
    row_count, model_width = raw_keys.shape
    by_head = raw_keys.reshape(row_count, HEADS, model_width // HEADS)
    shrink = lax.rsqrt(jnp.mean(by_head * by_head, axis=-1, keepdims=True) + 1e-06)
    return ((by_head * shrink).reshape(row_count, model_width) * key_gain).astype(BF16)


def encode_user(history_rows, user_query, user_length, key_weight, key_gain, interest_gain):
    seq_len, model_width = history_rows.shape
    head_dim = model_width // HEADS
    key_block = key_rows(history_rows, key_weight, key_gain)
    query_heads = user_query.reshape(user_query.shape[0], HEADS, head_dim)
    key_heads = key_block.reshape(seq_len, HEADS, head_dim)
    scores = jnp.einsum(
        "qhd,lhd->hql", query_heads, key_heads, preferred_element_type=F32
    ) / math.sqrt(head_dim)
    live_mask = lax.broadcasted_iota(jnp.int32, (1, 1, seq_len), 2) < user_length
    scores = jnp.where(live_mask, scores, -1e30)
    row_max = jnp.max(scores, axis=-1, keepdims=True)
    expo = jnp.exp(scores - row_max)
    attention = (expo / jnp.sum(expo, axis=-1, keepdims=True)).astype(BF16)
    value_heads = history_rows.reshape(seq_len, HEADS, head_dim)
    pooled = jnp.einsum("hql,lhd->qhd", attention, value_heads, preferred_element_type=F32)
    pieces = pooled.reshape(user_query.shape[0], model_width // EMB, EMB)
    norm_inv = lax.rsqrt(jnp.mean(pieces * pieces, axis=-1, keepdims=True) + 1e-06)
    normed = pieces * norm_inv * interest_gain
    return normed.reshape(user_query.shape[0] * (model_width // EMB), EMB).astype(BF16)


def pack_kernel(rows_ref, *refs):
    inputs, (out_ref, scratch), (held, arrived) = refs[:6], refs[6:8], (refs[8:14], refs[14])
    copies = [
        pltpu.make_async_copy(source, target, arrived.at[i])
        for i, (source, target) in enumerate(zip(inputs, held))
    ]
    for copy in copies:
        copy.start()
    for copy in copies:
        copy.wait()
    wanted_ref, sparse_ref, cot_int_ref, cot_spa_ref, proj_int_ref, proj_spa_ref = held
    devices, width = out_ref.shape[0], sparse_ref.shape[1]
    batch = sparse_ref.shape[0]
    for user in range(2 * devices):
        lanes = slice((user % 2) * EMB, (user % 2 + 1) * EMB)
        out_ref[user // 2, :, lanes] = sparse_ref[rows_ref[0, user]]
    row_of = lax.broadcasted_iota(jnp.int32, (batch, batch), 0)
    pick = (row_of == wanted_ref[...]).astype(BF16)
    for j in range(width):
        cots = jnp.concatenate([cot_int_ref[:, j, :], cot_spa_ref[:, j, :]], axis=0)
        scratch[:, :STATE] = lax.dot_general(
            pick, cots, (((0,), (1,)), ((), ())), preferred_element_type=F32
        )
        proj = jnp.concatenate([proj_int_ref[j : j + 1, :], proj_spa_ref[j : j + 1, :]], axis=1)
        parts = [scratch[pl.ds(slot, devices, stride=2), :STATE] for slot in range(2)]
        parts.append(jnp.broadcast_to(proj.astype(F32), (devices, STATE)))
        parts.append(jnp.zeros((devices, 128 - 3 * STATE), F32))
        out_ref[:, j, SIDE:] = jnp.concatenate(parts, axis=1).astype(BF16)


def pack(assignment, sparse_embed, cots, projs):
    batch, width, _ = sparse_embed.shape
    inputs = [
        pltpu.with_memory_space_constraint(array, pltpu.HBM)
        for array in (assignment, sparse_embed, *cots, *projs)
    ]
    return pl.pallas_call(
        pack_kernel,
        out_shape=jax.ShapeDtypeStruct((batch // 2, width, PACKED), BF16),
        in_specs=[pl.BlockSpec(memory_space=pltpu.SMEM)]
        + [pl.BlockSpec(memory_space=pltpu.HBM)] * len(inputs),
        out_specs=pl.BlockSpec(memory_space=pltpu.VMEM),
        scratch_shapes=[pltpu.VMEM((batch, 128), F32)]
        + [pltpu.VMEM(array.shape, array.dtype) for array in inputs]
        + [pltpu.SemaphoreType.DMA((len(inputs),))],
        compiler_params=pltpu.CompilerParams(vmem_limit_bytes=32 * 2**20),
        name="pack_rows",
    )(assignment, *inputs)


def state_kernel(factor, packed_ref, interest_ref, sent_ref):
    contract_rows = (((0,), (0,)), ((), ()))
    contract_lanes = (((1,), (1,)), ((), ()))
    side = packed_ref[:, SIDE:]
    proj = side[:, 2 * STATE : 3 * STATE]
    total_int, total_spa = None, None
    for slot in range(2):
        interest = interest_ref[slot]
        sparse = packed_ref[:, slot * EMB : (slot + 1) * EMB]
        cot = side[:, slot * STATE : (slot + 1) * STATE]
        left_int = jnp.concatenate([proj[:, :RANK], cot[:, :RANK]], axis=1)
        left_spa = jnp.concatenate([proj[:, RANK:], cot[:, RANK:]], axis=1)
        summed = lax.dot_general(
            left_int, interest, contract_rows, preferred_element_type=F32
        ) + lax.dot_general(left_spa, sparse, contract_rows, preferred_element_type=F32)
        is_state = lax.broadcasted_iota(jnp.int32, summed.shape, 0) < RANK
        rounded = jnp.where(is_state, summed, summed * factor).astype(BF16)
        sent_ref[slot] = rounded
        grad = rounded[RANK:, :]
        part_int = lax.dot_general(grad, interest, contract_lanes, preferred_element_type=F32)
        part_spa = lax.dot_general(grad, sparse, contract_lanes, preferred_element_type=F32)
        total_int = part_int if total_int is None else total_int + part_int
        total_spa = part_spa if total_spa is None else total_spa + part_spa
    sent_ref[2] = jnp.concatenate([total_int, total_spa], axis=0).astype(BF16)


def make_state(packed, interest):
    vmem = pl.BlockSpec(memory_space=pltpu.VMEM)
    return pl.pallas_call(
        functools.partial(state_kernel, 1.0 / math.sqrt(EMB)),
        out_shape=jax.ShapeDtypeStruct((3, STATE, EMB), BF16),
        in_specs=[vmem, vmem],
        out_specs=vmem,
        compiler_params=pltpu.CompilerParams(vmem_limit_bytes=32 * 2**20),
        name="make_state",
    )(packed, interest)


def split_kernel(shards, block_ref, got_ref, state_ref, spread_ref):
    total = None
    for source in range(state_ref.shape[0]):
        for slot in range(2):
            state_ref[source, slot * STATE : (slot + 1) * STATE, :] = got_ref[3 * source + slot]
        part = got_ref[3 * source + 2].astype(F32)
        total = part if total is None else total + part
    total = jnp.concatenate([total, jnp.zeros((128 - STATE, total.shape[1]), F32)], axis=0)
    width = spread_ref.shape[1]
    halves = 2
    columns = total.shape[1] // halves
    for half in range(halves):
        mine = pltpu.roll(
            total[:, half * columns : (half + 1) * columns],
            columns - block_ref[0] * PAIR * width,
            1,
        )
        turned = jnp.transpose(mine)
        for member in range(PAIR):
            row = turned[member * width : (member + 1) * width, :]
            for shard in range(shards):
                spread_ref[(half * shards + shard) * PAIR + member] = row


def split_sums(block, gathered, shards, width):
    vmem = pl.BlockSpec(memory_space=pltpu.VMEM)
    sources, emb = gathered.shape[0] // 3, gathered.shape[2]
    return pl.pallas_call(
        functools.partial(split_kernel, shards),
        out_shape=(
            jax.ShapeDtypeStruct((sources, 2 * STATE, emb), BF16),
            jax.ShapeDtypeStruct((2 * shards * PAIR, width, 128), F32),
        ),
        in_specs=[pl.BlockSpec(memory_space=pltpu.SMEM), vmem],
        out_specs=(vmem, vmem),
        compiler_params=pltpu.CompilerParams(vmem_limit_bytes=32 * 2**20),
        name="split_sums",
    )(block, gathered)


def embed_kernel(rows_ref, left_int_ref, left_spa_ref, *refs):
    sources, (int_ref, spa_ref) = refs[:-2], refs[-2:]
    each = left_int_ref.shape[0] // len(sources)
    for block in range(left_int_ref.shape[0]):
        source = sources[block // each]
        first = (block % each) * NEAR
        states = source[first : first + NEAR].reshape(NEAR * 2 * STATE, EMB)
        got_int = jnp.dot(left_int_ref[block], states, preferred_element_type=F32)
        got_spa = jnp.dot(left_spa_ref[block], states, preferred_element_type=F32)
        for i in range(2 * NEAR):
            row = rows_ref[block * 2 * NEAR + i]
            int_ref[row] = got_int[8 * i : 8 * i + 4, :].astype(BF16)
            spa_ref[row] = got_spa[8 * i : 8 * i + 4, :].astype(BF16)


def embed_grads(rows, left_int, left_spa, sources, width):
    vmem = pl.BlockSpec(memory_space=pltpu.VMEM)
    out = jax.ShapeDtypeStruct((rows.shape[0], width, EMB), BF16)
    return pl.pallas_call(
        embed_kernel,
        out_shape=(out, out),
        in_specs=[pl.BlockSpec(memory_space=pltpu.SMEM)] + [vmem] * (2 + len(sources)),
        out_specs=(vmem, vmem),
        compiler_params=pltpu.CompilerParams(vmem_limit_bytes=32 * 2**20),
        name="embed_grads",
    )(rows, left_int, left_spa, *sources)


def left_kernel(
    factor, wanted_ref, cot_int_ref, cot_spa_ref, proj_int_ref, proj_spa_ref, left_int_ref, left_spa_ref, rows
):
    blocks, height, depth = left_int_ref.shape
    users, width = wanted_ref.shape[1], proj_int_ref.shape[0]
    row_of = lax.broadcasted_iota(jnp.int32, (users, users), 0)
    pick = (row_of == wanted_ref[...]).astype(BF16)
    same = lax.broadcasted_iota(jnp.int32, (STATE, STATE), 0) == lax.broadcasted_iota(
        jnp.int32, (STATE, STATE), 1
    )
    repeat = jnp.concatenate([same.astype(BF16)] * (depth // STATE), axis=1)
    owner = lax.broadcasted_iota(jnp.int32, (height, STATE), 0) // 8
    mask = jnp.concatenate([(owner == i).astype(F32) for i in range(depth // STATE)], axis=1)
    for cot_ref, proj_ref, left_ref in (
        (cot_int_ref, proj_int_ref, left_int_ref),
        (cot_spa_ref, proj_spa_ref, left_spa_ref),
    ):
        rows[...] = jnp.zeros_like(rows)
        for j in range(width):
            cot = lax.dot_general(
                pick, cot_ref[:, j, :], (((0,), (1,)), ((), ())), preferred_element_type=F32
            )
            proj = jnp.broadcast_to(proj_ref[j : j + 1, :].astype(F32), (users, RANK))
            row = [cot * factor, proj, jnp.zeros((users, 128 - STATE), F32)]
            rows[pl.ds(j, users, stride=8), :] = jnp.concatenate(row, axis=1)
        for block in range(blocks):
            narrow = rows[block * height : (block + 1) * height, :STATE].astype(BF16)
            wide = jnp.dot(narrow, repeat, preferred_element_type=F32)
            left_ref[block] = (wide * mask).astype(BF16)


def left_blocks(wanted, cots, projs, factor):
    vmem = pl.BlockSpec(memory_space=pltpu.VMEM)
    users = wanted.shape[1]
    per_block = 2 * NEAR
    out = jax.ShapeDtypeStruct((users // per_block, per_block * 8, per_block * STATE), BF16)
    return pl.pallas_call(
        functools.partial(left_kernel, factor),
        out_shape=(out, out),
        in_specs=[vmem] * 5,
        out_specs=(vmem, vmem),
        scratch_shapes=[pltpu.VMEM((users * 8, 128), F32)],
        compiler_params=pltpu.CompilerParams(vmem_limit_bytes=32 * 2**20),
        name="left_blocks",
    )(wanted, *cots, *projs)


def on_device(
    history,
    queries,
    lengths,
    assignment,
    key_weight,
    key_gain,
    interest_gain,
    sparse_embed,
    proj_interest,
    proj_sparse,
    cot_interest,
    cot_sparse,
):
    batch_rows = assignment[0]
    batch_local, width, _ = sparse_embed.shape
    devices = batch_local // 2
    tensor = lax.axis_size("tensor")
    halves = lax.axis_size("half")
    factor = 1.0 / math.sqrt(EMB)

    cots = [cot_interest.transpose(2, 1, 0), cot_sparse.transpose(2, 1, 0)]
    packed = pack(assignment, sparse_embed, cots, [proj_interest, proj_sparse])
    arrived = lax.all_to_all(packed, ALL, split_axis=0, concat_axis=0, tiled=True)

    user_count = history.shape[1]
    encoded = [
        encode_user(
            history[0, user_slot],
            queries[0, user_slot],
            lengths[0, user_slot],
            key_weight,
            key_gain,
            interest_gain,
        )
        for user_slot in range(user_count)
    ]
    interest = jnp.stack(encoded, axis=0)

    far_count = tensor // PAIR
    far_groups = [[i + PAIR * m for m in range(far_count)] for i in range(PAIR)]
    my_half = lax.axis_index("half")
    my_tensor = lax.axis_index("tensor")
    tables = batch_rows.reshape(halves, far_count, PAIR, 2).transpose(0, 2, 1, 3)
    tables = jnp.where(my_half == 0, tables, tables[::-1])
    tables = jnp.where(my_tensor % PAIR == 0, tables, tables[:, ::-1])
    ordered_rows = tables.reshape(batch_local)
    left_int, left_spa = left_blocks(
        ordered_rows[None], cots, [proj_interest, proj_sparse], factor
    )
    interest, left_int, left_spa = lax.optimization_barrier((interest, left_int, left_spa))

    sent = make_state(arrived.reshape(devices * width, PACKED), interest)
    gathered = lax.all_gather(sent, "tensor", axis=0, tiled=True, axis_index_groups=far_groups)

    shards = lax.axis_size("dp")
    pair = my_tensor // PAIR
    far, spread = split_sums(pair.reshape(1).astype(jnp.int32), gathered, shards, width)
    across = [(i, (i + 1) % halves) for i in range(halves)]
    swap = [(i, i ^ 1) for i in range(tensor)]
    near = lax.ppermute(far, "tensor", swap)
    far_other = lax.ppermute(far, "half", across)
    near_other = lax.ppermute(near, "half", across)
    sum_groups = [
        [
            (half * shards + shard) * tensor + PAIR * m + i
            for half in range(halves)
            for shard in range(shards)
            for i in range(PAIR)
        ]
        for m in range(far_count)
    ]
    shares = lax.all_to_all(
        spread,
        ("half", "dp", "tensor"),
        split_axis=0,
        concat_axis=0,
        tiled=True,
        axis_index_groups=sum_groups,
    )
    batch_total = shards * batch_local
    proj_grads = jnp.sum(shares, axis=0)[:, :STATE] / batch_total

    grad_interest, grad_sparse = embed_grads(
        ordered_rows, left_int, left_spa, [far, near, far_other, near_other], width
    )
    return (grad_interest, grad_sparse, proj_grads[:, :RANK], proj_grads[:, RANK:])


def solution(mesh):
    placed = (
        P("dp", ("half", "tensor"), None, None),
        P("dp", ("half", "tensor"), None, None),
        P("dp", ("half", "tensor")),
        P("dp", None),
        P(),
        P(),
        P(),
        P("dp", ("half", "tensor"), None),
        P(("half", "tensor"), None),
        P(("half", "tensor"), None),
        P("dp", ("half", "tensor"), None),
        P("dp", ("half", "tensor"), None),
    )
    return jax.shard_map(
        on_device,
        mesh=mesh,
        in_specs=placed,
        out_specs=(
            P("dp", ("half", "tensor"), None),
            P("dp", ("half", "tensor"), None),
            P(("half", "tensor"), None),
            P(("half", "tensor"), None),
        ),
        check_vma=False,
    )
```

```python
import functools
import math

import jax
import jax.numpy as jnp
from jax import lax
from jax.experimental import pallas as pl
from jax.experimental.pallas import tpu as pltpu
from jax.sharding import PartitionSpec as P

HEADS = 8
EMB = 256
RANK = 12
STATE = 2 * RANK
SIDE = 2 * EMB
PACKED = 2 * EMB + 128
NEAR = 4
PAIR = 2
MEMBERS = 4
ALL = ("half", "tensor")
F32 = jnp.float32
BF16 = jnp.bfloat16


def encode_kernel(lengths_ref, history_ref, query_ref, weight_ref, gain_ref, interest_gain_ref, out_ref, left, right):
    seq_len, model_width = history_ref.shape
    head_dim = model_width // HEADS
    raw_keys = jnp.dot(history_ref[...], weight_ref[...], preferred_element_type=F32)
    length = lengths_ref[0, pl.program_id(0)]
    live = lax.broadcasted_iota(jnp.int32, (query_ref.shape[0], seq_len), 1) < length
    pooled = []
    for head in range(HEADS):
        lanes = slice(head * head_dim, (head + 1) * head_dim)
        raw = raw_keys[:, lanes]
        shrink = lax.rsqrt(jnp.mean(raw * raw, axis=-1, keepdims=True) + 1e-06)
        keys = (raw * shrink * gain_ref[:, lanes]).astype(BF16)
        scores = lax.dot_general(
            query_ref[:, lanes], keys, (((1,), (1,)), ((), ())), preferred_element_type=F32
        ) / math.sqrt(head_dim)
        scores = jnp.where(live, scores, -1e30)
        expo = jnp.exp(scores - jnp.max(scores, axis=-1, keepdims=True))
        attention = (expo / jnp.sum(expo, axis=-1, keepdims=True)).astype(BF16)
        pooled.append(jnp.dot(attention, history_ref[:, lanes], preferred_element_type=F32))
    heads_each = EMB // head_dim
    count = HEADS // heads_each
    for c in range(count):
        piece = jnp.concatenate(pooled[c * heads_each : (c + 1) * heads_each], axis=1)
        norm_inv = lax.rsqrt(jnp.mean(piece * piece, axis=-1, keepdims=True) + 1e-06)
        normed = piece * norm_inv * interest_gain_ref[...]
        rows = pl.ds(c, query_ref.shape[0], stride=count)
        left[rows, :] = normed[:, : EMB // 2]
        right[rows, :] = normed[:, EMB // 2 :]
    out_ref[...] = jnp.concatenate([left[...], right[...]], axis=1).astype(BF16)


def encode_users(history, queries, lengths, key_weight, key_gain, interest_gain):
    _, users, seq_len, model_width = history.shape
    query_count = queries.shape[2]
    rows = query_count * model_width // EMB

    def per_user(height, width):
        return pl.BlockSpec((None, None, height, width), lambda user: (0, user, 0, 0))

    def shared(height, width):
        return pl.BlockSpec((height, width), lambda user: (0, 0))

    return pl.pallas_call(
        encode_kernel,
        out_shape=jax.ShapeDtypeStruct((users, rows, EMB), BF16),
        grid=(users,),
        in_specs=[
            pl.BlockSpec(memory_space=pltpu.SMEM),
            per_user(seq_len, model_width),
            per_user(query_count, model_width),
            shared(model_width, model_width),
            shared(1, model_width),
            shared(1, EMB),
        ],
        out_specs=pl.BlockSpec((None, rows, EMB), lambda user: (user, 0, 0)),
        scratch_shapes=[pltpu.VMEM((rows, EMB // 2), F32)] * 2,
        compiler_params=pltpu.CompilerParams(vmem_limit_bytes=48 * 2**20),
        name="encode_users",
    )(lengths, history, queries, key_weight, key_gain[None], interest_gain[None])


def pack_kernel(rows_ref, *refs):
    inputs, (out_ref, scratch), (held, arrived) = refs[:6], refs[6:8], (refs[8:14], refs[14])
    copies = [
        pltpu.make_async_copy(source, target, arrived.at[i])
        for i, (source, target) in enumerate(zip(inputs, held))
    ]
    for copy in copies:
        copy.start()
    for copy in copies:
        copy.wait()
    wanted_ref, sparse_ref, cot_int_ref, cot_spa_ref, proj_int_ref, proj_spa_ref = held
    devices, width = out_ref.shape[0], sparse_ref.shape[1]
    batch = sparse_ref.shape[0]
    for user in range(2 * devices):
        lanes = slice((user % 2) * EMB, (user % 2 + 1) * EMB)
        out_ref[user // 2, :, lanes] = sparse_ref[rows_ref[0, user]]
    row_of = lax.broadcasted_iota(jnp.int32, (batch, batch), 0)
    pick = (row_of == wanted_ref[...]).astype(BF16)
    for j in range(width):
        cots = jnp.concatenate([cot_int_ref[:, j, :], cot_spa_ref[:, j, :]], axis=0)
        scratch[:, :STATE] = lax.dot_general(
            pick, cots, (((0,), (1,)), ((), ())), preferred_element_type=F32
        )
        proj = jnp.concatenate([proj_int_ref[j : j + 1, :], proj_spa_ref[j : j + 1, :]], axis=1)
        parts = [scratch[pl.ds(slot, devices, stride=2), :STATE] for slot in range(2)]
        parts.append(jnp.broadcast_to(proj.astype(F32), (devices, STATE)))
        parts.append(jnp.zeros((devices, 128 - 3 * STATE), F32))
        out_ref[:, j, SIDE:] = jnp.concatenate(parts, axis=1).astype(BF16)


def pack(assignment, sparse_embed, cots, projs):
    batch, width, _ = sparse_embed.shape
    inputs = [
        pltpu.with_memory_space_constraint(array, pltpu.HBM)
        for array in (assignment, sparse_embed, *cots, *projs)
    ]
    return pl.pallas_call(
        pack_kernel,
        out_shape=jax.ShapeDtypeStruct((batch // 2, width, PACKED), BF16),
        in_specs=[pl.BlockSpec(memory_space=pltpu.SMEM)]
        + [pl.BlockSpec(memory_space=pltpu.HBM)] * len(inputs),
        out_specs=pl.BlockSpec(memory_space=pltpu.VMEM),
        scratch_shapes=[pltpu.VMEM((batch, 128), F32)]
        + [pltpu.VMEM(array.shape, array.dtype) for array in inputs]
        + [pltpu.SemaphoreType.DMA((len(inputs),))],
        compiler_params=pltpu.CompilerParams(vmem_limit_bytes=32 * 2**20),
        name="pack_rows",
    )(assignment, *inputs)


def state_kernel(factor, packed_ref, interest_ref, sent_ref):
    contract_rows = (((0,), (0,)), ((), ()))
    contract_lanes = (((1,), (1,)), ((), ()))
    side = packed_ref[:, SIDE:]
    proj = side[:, 2 * STATE : 3 * STATE]
    total_int, total_spa = None, None
    for slot in range(2):
        interest = interest_ref[slot]
        sparse = packed_ref[:, slot * EMB : (slot + 1) * EMB]
        cot = side[:, slot * STATE : (slot + 1) * STATE]
        left_int = jnp.concatenate([proj[:, :RANK], cot[:, :RANK]], axis=1)
        left_spa = jnp.concatenate([proj[:, RANK:], cot[:, RANK:]], axis=1)
        summed = lax.dot_general(
            left_int, interest, contract_rows, preferred_element_type=F32
        ) + lax.dot_general(left_spa, sparse, contract_rows, preferred_element_type=F32)
        is_state = lax.broadcasted_iota(jnp.int32, summed.shape, 0) < RANK
        rounded = jnp.where(is_state, summed, summed * factor).astype(BF16)
        sent_ref[slot] = rounded
        grad = rounded[RANK:, :]
        part_int = lax.dot_general(grad, interest, contract_lanes, preferred_element_type=F32)
        part_spa = lax.dot_general(grad, sparse, contract_lanes, preferred_element_type=F32)
        total_int = part_int if total_int is None else total_int + part_int
        total_spa = part_spa if total_spa is None else total_spa + part_spa
    sent_ref[2] = jnp.concatenate([total_int, total_spa], axis=0).astype(BF16)


def make_state(packed, interest):
    vmem = pl.BlockSpec(memory_space=pltpu.VMEM)
    return pl.pallas_call(
        functools.partial(state_kernel, 1.0 / math.sqrt(EMB)),
        out_shape=jax.ShapeDtypeStruct((3, STATE, EMB), BF16),
        in_specs=[vmem, vmem],
        out_specs=vmem,
        compiler_params=pltpu.CompilerParams(vmem_limit_bytes=32 * 2**20),
        name="make_state",
    )(packed, interest)


def columns_kernel(factor, wanted_ref, cot_int_ref, cot_spa_ref, proj_int_ref, proj_spa_ref, out_ref, rows):
    users, width = wanted_ref.shape[1], proj_int_ref.shape[0]
    row_of = lax.broadcasted_iota(jnp.int32, (users, users), 0)
    pick = (row_of == wanted_ref[...]).astype(BF16)
    for kind, (cot_ref, proj_ref) in enumerate(
        ((cot_int_ref, proj_int_ref), (cot_spa_ref, proj_spa_ref))
    ):
        for j in range(width):
            cot = lax.dot_general(
                pick, cot_ref[:, j, :], (((0,), (1,)), ((), ())), preferred_element_type=F32
            )
            proj = jnp.broadcast_to(proj_ref[j : j + 1, :].astype(F32), (users, RANK))
            row = [cot * factor, proj, jnp.zeros((users, 128 - STATE), F32)]
            rows[pl.ds(kind * width + j, users, stride=8), :] = jnp.concatenate(row, axis=1)
    height = out_ref.shape[2]
    for member in range(out_ref.shape[0]):
        turned = jnp.transpose(rows[member * height : (member + 1) * height, :])
        out_ref[member] = turned[:STATE, :].astype(BF16)


def left_columns(wanted, cots, projs, factor):
    vmem = pl.BlockSpec(memory_space=pltpu.VMEM)
    users = wanted.shape[1]
    return pl.pallas_call(
        functools.partial(columns_kernel, factor),
        out_shape=jax.ShapeDtypeStruct((MEMBERS, STATE, users * 8 // MEMBERS), BF16),
        in_specs=[vmem] * 5,
        out_specs=vmem,
        scratch_shapes=[pltpu.VMEM((users * 8, 128), F32)],
        compiler_params=pltpu.CompilerParams(vmem_limit_bytes=32 * 2**20),
        name="left_columns",
    )(wanted, *cots, *projs)


def left_kernel(*refs):
    columns, left_ref = refs[:-1], refs[-1]
    blocks, height, depth = left_ref.shape[1:]
    same = lax.broadcasted_iota(jnp.int32, (STATE, STATE), 0) == lax.broadcasted_iota(
        jnp.int32, (STATE, STATE), 1
    )
    repeat = jnp.concatenate([same.astype(BF16)] * (depth // STATE), axis=1)
    owner = lax.broadcasted_iota(jnp.int32, (height, STATE), 0) // 8
    mask = jnp.concatenate([(owner == i).astype(F32) for i in range(depth // STATE)], axis=1)
    for member, column_ref in enumerate(columns):
        wide = lax.dot_general(
            column_ref[...], repeat, (((0,), (0,)), ((), ())), preferred_element_type=F32
        )
        for block in range(blocks):
            part = wide[block * height : (block + 1) * height, :]
            left_ref[member, block] = (part * mask).astype(BF16)


def left_blocks(columns):
    vmem = pl.BlockSpec(memory_space=pltpu.VMEM)
    per_block = 2 * NEAR
    height = per_block * 8
    blocks = columns[0].shape[1] // height
    return pl.pallas_call(
        left_kernel,
        out_shape=jax.ShapeDtypeStruct((len(columns), blocks, height, per_block * STATE), BF16),
        in_specs=[vmem] * len(columns),
        out_specs=vmem,
        compiler_params=pltpu.CompilerParams(vmem_limit_bytes=32 * 2**20),
        name="left_blocks",
    )(*columns)


def embed_kernel(shards, place_ref, left_ref, got_ref, *refs):
    outs, spread_ref, states = refs[:MEMBERS], refs[MEMBERS], refs[MEMBERS + 1]
    total = None
    for source in range(states.shape[0]):
        for slot in range(2):
            states[source, slot * STATE : (slot + 1) * STATE, :] = got_ref[3 * source + slot]
        part = got_ref[3 * source + 2].astype(F32)
        total = part if total is None else total + part
    total = jnp.concatenate([total, jnp.zeros((128 - STATE, total.shape[1]), F32)], axis=0)
    width = spread_ref.shape[1]
    halves = 2
    columns = total.shape[1] // halves
    for half in range(halves):
        mine = pltpu.roll(
            total[:, half * columns : (half + 1) * columns],
            columns - place_ref[0] * PAIR * width,
            1,
        )
        turned = jnp.transpose(mine)
        for member in range(PAIR):
            row = turned[member * width : (member + 1) * width, :]
            for shard in range(shards):
                spread_ref[(half * shards + shard) * PAIR + member] = row
    for block in range(left_ref.shape[1]):
        right = states[block * NEAR : (block + 1) * NEAR].reshape(NEAR * 2 * STATE, EMB)
        for member, out_ref in enumerate(outs):
            got = jnp.dot(left_ref[member, block], right, preferred_element_type=F32)
            for i in range(2 * NEAR):
                out_ref[block * 2 * NEAR + i] = got[8 * i : 8 * i + 8, :].astype(BF16)


def embed_rows(place, left, gathered, shards, width):
    vmem = pl.BlockSpec(memory_space=pltpu.VMEM)
    sources, emb = gathered.shape[0] // 3, gathered.shape[2]
    out = jax.ShapeDtypeStruct((2 * sources, 8, emb), BF16)
    return pl.pallas_call(
        functools.partial(embed_kernel, shards),
        out_shape=(out,) * MEMBERS
        + (jax.ShapeDtypeStruct((2 * shards * PAIR, width, 128), F32),),
        in_specs=[pl.BlockSpec(memory_space=pltpu.SMEM), vmem, vmem],
        out_specs=(vmem,) * (MEMBERS + 1),
        scratch_shapes=[pltpu.VMEM((sources, 2 * STATE, emb), BF16)],
        compiler_params=pltpu.CompilerParams(vmem_limit_bytes=32 * 2**20),
        name="embed_rows",
    )(place, left, gathered)


def scatter_kernel(rows_ref, *refs):
    sources, (int_ref, spa_ref) = refs[:-2], refs[-2:]
    width = int_ref.shape[1]
    for member, source in enumerate(sources):
        users = source.shape[0]
        for user in range(users):
            row = rows_ref[member * users + user]
            both = source[user].astype(F32)
            int_ref[row] = both[:width, :].astype(BF16)
            spa_ref[row] = both[width:, :].astype(BF16)


def scatter_rows(rows, sources, width):
    vmem = pl.BlockSpec(memory_space=pltpu.VMEM)
    out = jax.ShapeDtypeStruct((rows.shape[0], width, EMB), BF16)
    return pl.pallas_call(
        scatter_kernel,
        out_shape=(out, out),
        in_specs=[pl.BlockSpec(memory_space=pltpu.SMEM)] + [vmem] * len(sources),
        out_specs=(vmem, vmem),
        compiler_params=pltpu.CompilerParams(vmem_limit_bytes=32 * 2**20),
        name="scatter_rows",
    )(rows, *sources)


def on_device(
    history,
    queries,
    lengths,
    assignment,
    key_weight,
    key_gain,
    interest_gain,
    sparse_embed,
    proj_interest,
    proj_sparse,
    cot_interest,
    cot_sparse,
):
    batch_rows = assignment[0]
    batch_local, width, _ = sparse_embed.shape
    devices = batch_local // 2
    tensor = lax.axis_size("tensor")
    halves = lax.axis_size("half")
    factor = 1.0 / math.sqrt(EMB)

    cots = [cot_interest.transpose(2, 1, 0), cot_sparse.transpose(2, 1, 0)]
    packed = pack(assignment, sparse_embed, cots, [proj_interest, proj_sparse])
    arrived = lax.all_to_all(packed, ALL, split_axis=0, concat_axis=0, tiled=True)

    interest = encode_users(history, queries, lengths, key_weight, key_gain, interest_gain)

    far_count = tensor // PAIR
    far_groups = [[i + PAIR * m for m in range(far_count)] for i in range(PAIR)]
    my_half = lax.axis_index("half")
    my_tensor = lax.axis_index("tensor")
    tables = batch_rows.reshape(halves, far_count, PAIR, 2).transpose(0, 2, 1, 3)
    tables = jnp.where(my_half == 0, tables, tables[::-1])
    tables = jnp.where(my_tensor % PAIR == 0, tables, tables[:, ::-1])
    ordered_rows = tables.reshape(batch_local)
    flips = [
        [(h * tensor + z, (h ^ over_half) * tensor + (z ^ over_pair)) for h in range(halves) for z in range(tensor)]
        for over_half in range(halves)
        for over_pair in range(PAIR)
    ]
    wanted, interest = lax.optimization_barrier((ordered_rows[None], interest))
    columns = left_columns(wanted, cots, [proj_interest, proj_sparse], factor)
    left = left_blocks(
        [columns[0]] + [lax.ppermute(columns[i], ALL, flips[i]) for i in range(1, MEMBERS)]
    )
    interest, left = lax.optimization_barrier((interest, left))

    sent = make_state(arrived.reshape(devices * width, PACKED), interest)
    gathered = lax.all_gather(sent, "tensor", axis=0, tiled=True, axis_index_groups=far_groups)

    shards = lax.axis_size("dp")
    pair = my_tensor // PAIR
    *outs, spread = embed_rows(
        pair.reshape(1).astype(jnp.int32), left, gathered, shards, width
    )
    sum_groups = [
        [
            (half * shards + shard) * tensor + PAIR * m + i
            for half in range(halves)
            for shard in range(shards)
            for i in range(PAIR)
        ]
        for m in range(far_count)
    ]
    shares = lax.all_to_all(
        spread,
        ("half", "dp", "tensor"),
        split_axis=0,
        concat_axis=0,
        tiled=True,
        axis_index_groups=sum_groups,
    )
    batch_total = shards * batch_local
    proj_grads = jnp.sum(shares, axis=0)[:, :STATE] / batch_total

    crossed = {i: lax.ppermute(outs[i], ALL, flips[i]) for i in (3, 1, 2)}
    sources = [outs[0]] + [crossed[i] for i in range(1, MEMBERS)]
    grad_interest, grad_sparse = scatter_rows(ordered_rows, sources, width)
    return (grad_interest, grad_sparse, proj_grads[:, :RANK], proj_grads[:, RANK:])


def solution(mesh):
    placed = (
        P("dp", ("half", "tensor"), None, None),
        P("dp", ("half", "tensor"), None, None),
        P("dp", ("half", "tensor")),
        P("dp", None),
        P(),
        P(),
        P(),
        P("dp", ("half", "tensor"), None),
        P(("half", "tensor"), None),
        P(("half", "tensor"), None),
        P("dp", ("half", "tensor"), None),
        P("dp", ("half", "tensor"), None),
    )
    return jax.shard_map(
        on_device,
        mesh=mesh,
        in_specs=placed,
        out_specs=(
            P("dp", ("half", "tensor"), None),
            P("dp", ("half", "tensor"), None),
            P(("half", "tensor"), None),
            P(("half", "tensor"), None),
        ),
        check_vma=False,
    )
```

```python
import functools
import math

import jax
import jax.numpy as jnp
from jax import lax
from jax.experimental import pallas as pl
from jax.experimental.pallas import tpu as pltpu
from jax.sharding import PartitionSpec as P

HEADS = 8
EMB = 256
RANK = 12
STATE = 2 * RANK
SIDE = 2 * EMB
PACKED = 2 * EMB + 128
NEAR = 4
PAIR = 2
MEMBERS = 4
ALL = ("half", "tensor")
F32 = jnp.float32
BF16 = jnp.bfloat16


def encode_kernel(lengths_ref, history_ref, query_ref, weight_ref, gain_ref, interest_gain_ref, out_ref, left, right):
    seq_len, model_width = history_ref.shape
    head_dim = model_width // HEADS
    raw_keys = jnp.dot(history_ref[...], weight_ref[...], preferred_element_type=F32)
    length = lengths_ref[0, pl.program_id(0)]
    live = lax.broadcasted_iota(jnp.int32, (query_ref.shape[0], seq_len), 1) < length
    pooled = []
    for head in range(HEADS):
        lanes = slice(head * head_dim, (head + 1) * head_dim)
        raw = raw_keys[:, lanes]
        shrink = lax.rsqrt(jnp.mean(raw * raw, axis=-1, keepdims=True) + 1e-06)
        keys = (raw * shrink * gain_ref[:, lanes]).astype(BF16)
        scores = lax.dot_general(
            query_ref[:, lanes], keys, (((1,), (1,)), ((), ())), preferred_element_type=F32
        ) / math.sqrt(head_dim)
        scores = jnp.where(live, scores, -1e30)
        expo = jnp.exp(scores - jnp.max(scores, axis=-1, keepdims=True))
        attention = (expo / jnp.sum(expo, axis=-1, keepdims=True)).astype(BF16)
        pooled.append(jnp.dot(attention, history_ref[:, lanes], preferred_element_type=F32))
    heads_each = EMB // head_dim
    count = HEADS // heads_each
    for c in range(count):
        piece = jnp.concatenate(pooled[c * heads_each : (c + 1) * heads_each], axis=1)
        norm_inv = lax.rsqrt(jnp.mean(piece * piece, axis=-1, keepdims=True) + 1e-06)
        normed = piece * norm_inv * interest_gain_ref[...]
        rows = pl.ds(c, query_ref.shape[0], stride=count)
        left[rows, :] = normed[:, : EMB // 2]
        right[rows, :] = normed[:, EMB // 2 :]
    out_ref[...] = jnp.concatenate([left[...], right[...]], axis=1).astype(BF16)


def encode_users(history, queries, lengths, key_weight, key_gain, interest_gain):
    _, users, seq_len, model_width = history.shape
    query_count = queries.shape[2]
    rows = query_count * model_width // EMB

    def per_user(height, width):
        return pl.BlockSpec((None, None, height, width), lambda user: (0, user, 0, 0))

    def shared(height, width):
        return pl.BlockSpec((height, width), lambda user: (0, 0))

    return pl.pallas_call(
        encode_kernel,
        out_shape=jax.ShapeDtypeStruct((users, rows, EMB), BF16),
        grid=(users,),
        in_specs=[
            pl.BlockSpec(memory_space=pltpu.SMEM),
            per_user(seq_len, model_width),
            per_user(query_count, model_width),
            shared(model_width, model_width),
            shared(1, model_width),
            shared(1, EMB),
        ],
        out_specs=pl.BlockSpec((None, rows, EMB), lambda user: (user, 0, 0)),
        scratch_shapes=[pltpu.VMEM((rows, EMB // 2), F32)] * 2,
        compiler_params=pltpu.CompilerParams(vmem_limit_bytes=48 * 2**20),
        name="encode_users",
    )(lengths, history, queries, key_weight, key_gain[None], interest_gain[None])


def pack_kernel(rows_ref, *refs):
    inputs, (out_ref, scratch), (held, arrived) = refs[:6], refs[6:8], (refs[8:14], refs[14])
    copies = [
        pltpu.make_async_copy(source, target, arrived.at[i])
        for i, (source, target) in enumerate(zip(inputs, held))
    ]
    for copy in copies:
        copy.start()
    for copy in copies:
        copy.wait()
    wanted_ref, sparse_ref, cot_int_ref, cot_spa_ref, proj_int_ref, proj_spa_ref = held
    devices, width = out_ref.shape[0], sparse_ref.shape[1]
    batch = sparse_ref.shape[0]
    for user in range(2 * devices):
        lanes = slice((user % 2) * EMB, (user % 2 + 1) * EMB)
        out_ref[user // 2, :, lanes] = sparse_ref[rows_ref[0, user]]
    row_of = lax.broadcasted_iota(jnp.int32, (batch, batch), 0)
    pick = (row_of == wanted_ref[...]).astype(BF16)
    for j in range(width):
        cots = jnp.concatenate([cot_int_ref[:, j, :], cot_spa_ref[:, j, :]], axis=0)
        scratch[:, :STATE] = lax.dot_general(
            pick, cots, (((0,), (1,)), ((), ())), preferred_element_type=F32
        )
        proj = jnp.concatenate([proj_int_ref[j : j + 1, :], proj_spa_ref[j : j + 1, :]], axis=1)
        parts = [scratch[pl.ds(slot, devices, stride=2), :STATE] for slot in range(2)]
        parts.append(jnp.broadcast_to(proj.astype(F32), (devices, STATE)))
        parts.append(jnp.zeros((devices, 128 - 3 * STATE), F32))
        out_ref[:, j, SIDE:] = jnp.concatenate(parts, axis=1).astype(BF16)


def pack(assignment, sparse_embed, cots, projs):
    batch, width, _ = sparse_embed.shape
    inputs = [
        pltpu.with_memory_space_constraint(array, pltpu.HBM)
        for array in (assignment, sparse_embed, *cots, *projs)
    ]
    return pl.pallas_call(
        pack_kernel,
        out_shape=jax.ShapeDtypeStruct((batch // 2, width, PACKED), BF16),
        in_specs=[pl.BlockSpec(memory_space=pltpu.SMEM)]
        + [pl.BlockSpec(memory_space=pltpu.HBM)] * len(inputs),
        out_specs=pl.BlockSpec(memory_space=pltpu.VMEM),
        scratch_shapes=[pltpu.VMEM((batch, 128), F32)]
        + [pltpu.VMEM(array.shape, array.dtype) for array in inputs]
        + [pltpu.SemaphoreType.DMA((len(inputs),))],
        compiler_params=pltpu.CompilerParams(vmem_limit_bytes=32 * 2**20),
        name="pack_rows",
    )(assignment, *inputs)


def state_kernel(factor, packed_ref, interest_ref, sent_ref):
    contract_rows = (((0,), (0,)), ((), ()))
    contract_lanes = (((1,), (1,)), ((), ()))
    side = packed_ref[:, SIDE:]
    proj = side[:, 2 * STATE : 3 * STATE]
    total_int, total_spa = None, None
    for slot in range(2):
        interest = interest_ref[slot]
        sparse = packed_ref[:, slot * EMB : (slot + 1) * EMB]
        cot = side[:, slot * STATE : (slot + 1) * STATE]
        left_int = jnp.concatenate([proj[:, :RANK], cot[:, :RANK]], axis=1)
        left_spa = jnp.concatenate([proj[:, RANK:], cot[:, RANK:]], axis=1)
        summed = lax.dot_general(
            left_int, interest, contract_rows, preferred_element_type=F32
        ) + lax.dot_general(left_spa, sparse, contract_rows, preferred_element_type=F32)
        is_state = lax.broadcasted_iota(jnp.int32, summed.shape, 0) < RANK
        rounded = jnp.where(is_state, summed, summed * factor).astype(BF16)
        sent_ref[slot] = rounded
        grad = rounded[RANK:, :]
        part_int = lax.dot_general(grad, interest, contract_lanes, preferred_element_type=F32)
        part_spa = lax.dot_general(grad, sparse, contract_lanes, preferred_element_type=F32)
        total_int = part_int if total_int is None else total_int + part_int
        total_spa = part_spa if total_spa is None else total_spa + part_spa
    sent_ref[2] = jnp.concatenate([total_int, total_spa], axis=0).astype(BF16)


def make_state(packed, interest):
    vmem = pl.BlockSpec(memory_space=pltpu.VMEM)
    return pl.pallas_call(
        functools.partial(state_kernel, 1.0 / math.sqrt(EMB)),
        out_shape=jax.ShapeDtypeStruct((3, STATE, EMB), BF16),
        in_specs=[vmem, vmem],
        out_specs=vmem,
        compiler_params=pltpu.CompilerParams(vmem_limit_bytes=32 * 2**20),
        name="make_state",
    )(packed, interest)


def columns_kernel(factor, wanted_ref, cot_int_ref, cot_spa_ref, proj_int_ref, proj_spa_ref, out_ref, rows):
    users, width = wanted_ref.shape[1], proj_int_ref.shape[0]
    row_of = lax.broadcasted_iota(jnp.int32, (users, users), 0)
    pick = (row_of == wanted_ref[...]).astype(BF16)
    for kind, (cot_ref, proj_ref) in enumerate(
        ((cot_int_ref, proj_int_ref), (cot_spa_ref, proj_spa_ref))
    ):
        for j in range(width):
            cot = lax.dot_general(
                pick, cot_ref[:, j, :], (((0,), (1,)), ((), ())), preferred_element_type=F32
            )
            proj = jnp.broadcast_to(proj_ref[j : j + 1, :].astype(F32), (users, RANK))
            row = [cot * factor, proj, jnp.zeros((users, 128 - STATE), F32)]
            rows[pl.ds(kind * width + j, users, stride=8), :] = jnp.concatenate(row, axis=1)
    height = out_ref.shape[2]
    for member in range(out_ref.shape[0]):
        turned = jnp.transpose(rows[member * height : (member + 1) * height, :])
        out_ref[member] = turned[:STATE, :].astype(BF16)


def left_columns(wanted, cots, projs, factor):
    vmem = pl.BlockSpec(memory_space=pltpu.VMEM)
    users = wanted.shape[1]
    return pl.pallas_call(
        functools.partial(columns_kernel, factor),
        out_shape=jax.ShapeDtypeStruct((MEMBERS, STATE, users * 8 // MEMBERS), BF16),
        in_specs=[vmem] * 5,
        out_specs=vmem,
        scratch_shapes=[pltpu.VMEM((users * 8, 128), F32)],
        compiler_params=pltpu.CompilerParams(vmem_limit_bytes=32 * 2**20),
        name="left_columns",
    )(wanted, *cots, *projs)


def left_kernel(*refs):
    columns, left_ref = refs[:-1], refs[-1]
    blocks, height, depth = left_ref.shape[1:]
    same = lax.broadcasted_iota(jnp.int32, (STATE, STATE), 0) == lax.broadcasted_iota(
        jnp.int32, (STATE, STATE), 1
    )
    repeat = jnp.concatenate([same.astype(BF16)] * (depth // STATE), axis=1)
    owner = lax.broadcasted_iota(jnp.int32, (height, STATE), 0) // 8
    mask = jnp.concatenate([(owner == i).astype(F32) for i in range(depth // STATE)], axis=1)
    for member, column_ref in enumerate(columns):
        wide = lax.dot_general(
            column_ref[...], repeat, (((0,), (0,)), ((), ())), preferred_element_type=F32
        )
        for block in range(blocks):
            part = wide[block * height : (block + 1) * height, :]
            left_ref[member, block] = (part * mask).astype(BF16)


def left_blocks(columns):
    vmem = pl.BlockSpec(memory_space=pltpu.VMEM)
    per_block = 2 * NEAR
    height = per_block * 8
    blocks = columns[0].shape[1] // height
    return pl.pallas_call(
        left_kernel,
        out_shape=jax.ShapeDtypeStruct((len(columns), blocks, height, per_block * STATE), BF16),
        in_specs=[vmem] * len(columns),
        out_specs=vmem,
        compiler_params=pltpu.CompilerParams(vmem_limit_bytes=32 * 2**20),
        name="left_blocks",
    )(*columns)


def embed_kernel(shards, place_ref, left_ref, got_ref, *refs):
    outs, spread_ref, states = refs[:MEMBERS], refs[MEMBERS], refs[MEMBERS + 1]
    total = None
    for source in range(states.shape[0]):
        for slot in range(2):
            states[source, slot * STATE : (slot + 1) * STATE, :] = got_ref[3 * source + slot]
        part = got_ref[3 * source + 2].astype(F32)
        total = part if total is None else total + part
    total = jnp.concatenate([total, jnp.zeros((128 - STATE, total.shape[1]), F32)], axis=0)
    width = spread_ref.shape[1]
    halves = 2
    columns = total.shape[1] // halves
    for half in range(halves):
        mine = pltpu.roll(
            total[:, half * columns : (half + 1) * columns],
            columns - place_ref[0] * PAIR * width,
            1,
        )
        turned = jnp.transpose(mine)
        for member in range(PAIR):
            row = turned[member * width : (member + 1) * width, :]
            for shard in range(shards):
                spread_ref[(half * shards + shard) * PAIR + member] = row
    for block in range(left_ref.shape[1]):
        right = states[block * NEAR : (block + 1) * NEAR].reshape(NEAR * 2 * STATE, EMB)
        for member, out_ref in enumerate(outs):
            got = jnp.dot(left_ref[member, block], right, preferred_element_type=F32)
            for i in range(2 * NEAR):
                out_ref[block * 2 * NEAR + i] = got[8 * i : 8 * i + 8, :].astype(BF16)


def embed_rows(place, left, gathered, shards, width):
    vmem = pl.BlockSpec(memory_space=pltpu.VMEM)
    sources, emb = gathered.shape[0] // 3, gathered.shape[2]
    out = jax.ShapeDtypeStruct((2 * sources, 8, emb), BF16)
    return pl.pallas_call(
        functools.partial(embed_kernel, shards),
        out_shape=(out,) * MEMBERS
        + (jax.ShapeDtypeStruct((2 * shards * PAIR, width, 128), F32),),
        in_specs=[pl.BlockSpec(memory_space=pltpu.SMEM), vmem, vmem],
        out_specs=(vmem,) * (MEMBERS + 1),
        scratch_shapes=[pltpu.VMEM((sources, 2 * STATE, emb), BF16)],
        compiler_params=pltpu.CompilerParams(vmem_limit_bytes=32 * 2**20),
        name="embed_rows",
    )(place, left, gathered)


def scatter_kernel(rows_ref, *refs):
    sources, (int_ref, spa_ref) = refs[:-2], refs[-2:]
    width = int_ref.shape[1]
    for member, source in enumerate(sources):
        users = source.shape[0]
        for user in range(users):
            row = rows_ref[member * users + user]
            both = source[user].astype(F32)
            int_ref[row] = both[:width, :].astype(BF16)
            spa_ref[row] = both[width:, :].astype(BF16)


def scatter_rows(rows, sources, width):
    vmem = pl.BlockSpec(memory_space=pltpu.VMEM)
    out = jax.ShapeDtypeStruct((rows.shape[0], width, EMB), BF16)
    return pl.pallas_call(
        scatter_kernel,
        out_shape=(out, out),
        in_specs=[pl.BlockSpec(memory_space=pltpu.SMEM)] + [vmem] * len(sources),
        out_specs=(vmem, vmem),
        compiler_params=pltpu.CompilerParams(vmem_limit_bytes=32 * 2**20),
        name="scatter_rows",
    )(rows, *sources)


def on_device(
    history,
    queries,
    lengths,
    assignment,
    key_weight,
    key_gain,
    interest_gain,
    sparse_embed,
    proj_interest,
    proj_sparse,
    cot_interest,
    cot_sparse,
):
    batch_rows = assignment[0]
    batch_local, width, _ = sparse_embed.shape
    devices = batch_local // 2
    tensor = lax.axis_size("tensor")
    halves = lax.axis_size("half")
    factor = 1.0 / math.sqrt(EMB)

    cots = [cot_interest.transpose(2, 1, 0), cot_sparse.transpose(2, 1, 0)]
    packed = pack(assignment, sparse_embed, cots, [proj_interest, proj_sparse])
    arrived = lax.all_to_all(packed, ALL, split_axis=0, concat_axis=0, tiled=True)

    interest = encode_users(history, queries, lengths, key_weight, key_gain, interest_gain)

    far_count = tensor // PAIR
    far_groups = [[i + PAIR * m for m in range(far_count)] for i in range(PAIR)]
    my_half = lax.axis_index("half")
    my_tensor = lax.axis_index("tensor")
    tables = batch_rows.reshape(halves, far_count, PAIR, 2).transpose(0, 2, 1, 3)
    tables = jnp.where(my_half == 0, tables, tables[::-1])
    tables = jnp.where(my_tensor % PAIR == 0, tables, tables[:, ::-1])
    ordered_rows = tables.reshape(batch_local)
    flips = [
        [(h * tensor + z, (h ^ over_half) * tensor + (z ^ over_pair)) for h in range(halves) for z in range(tensor)]
        for over_half in range(halves)
        for over_pair in range(PAIR)
    ]
    wanted, interest = lax.optimization_barrier((ordered_rows[None], interest))
    columns = left_columns(wanted, cots, [proj_interest, proj_sparse], factor)
    left = left_blocks(
        [columns[0]] + [lax.ppermute(columns[i], ALL, flips[i]) for i in range(1, MEMBERS)]
    )
    interest, left = lax.optimization_barrier((interest, left))

    sent = make_state(arrived.reshape(devices * width, PACKED), interest)
    gathered = lax.all_gather(sent, "tensor", axis=0, tiled=True, axis_index_groups=far_groups)

    shards = lax.axis_size("dp")
    pair = my_tensor // PAIR
    *outs, spread = embed_rows(
        pair.reshape(1).astype(jnp.int32), left, gathered, shards, width
    )
    sum_groups = [
        [
            (half * shards + shard) * tensor + PAIR * m + i
            for half in range(halves)
            for shard in range(shards)
            for i in range(PAIR)
        ]
        for m in range(far_count)
    ]
    shares = lax.all_to_all(
        spread,
        ("half", "dp", "tensor"),
        split_axis=0,
        concat_axis=0,
        tiled=True,
        axis_index_groups=sum_groups,
    )
    batch_total = shards * batch_local
    proj_grads = jnp.sum(shares, axis=0)[:, :STATE] / batch_total

    sent_order = [3, 1, 2]
    sources = [outs[0]] + [lax.ppermute(outs[i], ALL, flips[i]) for i in sent_order]
    by_member = ordered_rows.reshape(MEMBERS, batch_local // MEMBERS)
    sent_rows = jnp.stack([by_member[i] for i in [0] + sent_order]).reshape(batch_local)
    grad_interest, grad_sparse = scatter_rows(sent_rows, sources, width)
    return (grad_interest, grad_sparse, proj_grads[:, :RANK], proj_grads[:, RANK:])


def solution(mesh):
    placed = (
        P("dp", ("half", "tensor"), None, None),
        P("dp", ("half", "tensor"), None, None),
        P("dp", ("half", "tensor")),
        P("dp", None),
        P(),
        P(),
        P(),
        P("dp", ("half", "tensor"), None),
        P(("half", "tensor"), None),
        P(("half", "tensor"), None),
        P("dp", ("half", "tensor"), None),
        P("dp", ("half", "tensor"), None),
    )
    return jax.shard_map(
        on_device,
        mesh=mesh,
        in_specs=placed,
        out_specs=(
            P("dp", ("half", "tensor"), None),
            P("dp", ("half", "tensor"), None),
            P(("half", "tensor"), None),
            P(("half", "tensor"), None),
        ),
        check_vma=False,
    )
```

```python
import functools
import math

import jax
import jax.numpy as jnp
from jax import lax
from jax.experimental import pallas as pl
from jax.experimental.pallas import tpu as pltpu
from jax.sharding import PartitionSpec as P

HEADS = 8
EMB = 256
RANK = 12
STATE = 2 * RANK
SIDE = 2 * EMB
PACKED = 2 * EMB + 128
NEAR = 4
PAIR = 2
MEMBERS = 4
ALL = ("half", "tensor")
F32 = jnp.float32
BF16 = jnp.bfloat16


def encode_kernel(lengths_ref, history_ref, query_ref, weight_ref, gain_ref, interest_gain_ref, out_ref, left, right):
    seq_len, model_width = history_ref.shape
    head_dim = model_width // HEADS
    raw_keys = jnp.dot(history_ref[...], weight_ref[...], preferred_element_type=F32)
    length = lengths_ref[0, pl.program_id(0)]
    live = lax.broadcasted_iota(jnp.int32, (query_ref.shape[0], seq_len), 1) < length
    pooled = []
    for head in range(HEADS):
        lanes = slice(head * head_dim, (head + 1) * head_dim)
        raw = raw_keys[:, lanes]
        shrink = lax.rsqrt(jnp.mean(raw * raw, axis=-1, keepdims=True) + 1e-06)
        keys = (raw * shrink * gain_ref[:, lanes]).astype(BF16)
        scores = lax.dot_general(
            query_ref[:, lanes], keys, (((1,), (1,)), ((), ())), preferred_element_type=F32
        ) / math.sqrt(head_dim)
        scores = jnp.where(live, scores, -1e30)
        expo = jnp.exp(scores - jnp.max(scores, axis=-1, keepdims=True))
        attention = (expo / jnp.sum(expo, axis=-1, keepdims=True)).astype(BF16)
        pooled.append(jnp.dot(attention, history_ref[:, lanes], preferred_element_type=F32))
    heads_each = EMB // head_dim
    count = HEADS // heads_each
    for c in range(count):
        piece = jnp.concatenate(pooled[c * heads_each : (c + 1) * heads_each], axis=1)
        norm_inv = lax.rsqrt(jnp.mean(piece * piece, axis=-1, keepdims=True) + 1e-06)
        normed = piece * norm_inv * interest_gain_ref[...]
        rows = pl.ds(c, query_ref.shape[0], stride=count)
        left[rows, :] = normed[:, : EMB // 2]
        right[rows, :] = normed[:, EMB // 2 :]
    out_ref[...] = jnp.concatenate([left[...], right[...]], axis=1).astype(BF16)


def encode_users(history, queries, lengths, key_weight, key_gain, interest_gain):
    _, users, seq_len, model_width = history.shape
    query_count = queries.shape[2]
    rows = query_count * model_width // EMB

    def per_user(height, width):
        return pl.BlockSpec((None, None, height, width), lambda user: (0, user, 0, 0))

    def shared(height, width):
        return pl.BlockSpec((height, width), lambda user: (0, 0))

    return pl.pallas_call(
        encode_kernel,
        out_shape=jax.ShapeDtypeStruct((users, rows, EMB), BF16),
        grid=(users,),
        in_specs=[
            pl.BlockSpec(memory_space=pltpu.SMEM),
            per_user(seq_len, model_width),
            per_user(query_count, model_width),
            shared(model_width, model_width),
            shared(1, model_width),
            shared(1, EMB),
        ],
        out_specs=pl.BlockSpec((None, rows, EMB), lambda user: (user, 0, 0)),
        scratch_shapes=[pltpu.VMEM((rows, EMB // 2), F32)] * 2,
        compiler_params=pltpu.CompilerParams(vmem_limit_bytes=48 * 2**20),
        name="encode_users",
    )(lengths, history, queries, key_weight, key_gain[None], interest_gain[None])


def pack_kernel(rows_ref, *refs):
    inputs, (out_ref, scratch), (held, arrived) = refs[:6], refs[6:8], (refs[8:14], refs[14])
    copies = [
        pltpu.make_async_copy(source, target, arrived.at[i])
        for i, (source, target) in enumerate(zip(inputs, held))
    ]
    for copy in copies:
        copy.start()
    for i in (0, 2, 3, 4, 5):
        copies[i].wait()
    wanted_ref, sparse_ref, cot_int_ref, cot_spa_ref, proj_int_ref, proj_spa_ref = held
    devices, width = out_ref.shape[0], sparse_ref.shape[1]
    batch = sparse_ref.shape[0]
    row_of = lax.broadcasted_iota(jnp.int32, (batch, batch), 0)
    pick = (row_of == wanted_ref[...]).astype(BF16)
    for j in range(width):
        cots = jnp.concatenate([cot_int_ref[:, j, :], cot_spa_ref[:, j, :]], axis=0)
        scratch[:, :STATE] = lax.dot_general(
            pick, cots, (((0,), (1,)), ((), ())), preferred_element_type=F32
        )
        proj = jnp.concatenate([proj_int_ref[j : j + 1, :], proj_spa_ref[j : j + 1, :]], axis=1)
        parts = [scratch[pl.ds(slot, devices, stride=2), :STATE] for slot in range(2)]
        parts.append(jnp.broadcast_to(proj.astype(F32), (devices, STATE)))
        parts.append(jnp.zeros((devices, 128 - 3 * STATE), F32))
        out_ref[:, j, SIDE:] = jnp.concatenate(parts, axis=1).astype(BF16)
    copies[1].wait()
    for user in range(2 * devices):
        lanes = slice((user % 2) * EMB, (user % 2 + 1) * EMB)
        out_ref[user // 2, :, lanes] = sparse_ref[rows_ref[0, user]]


def pack(assignment, sparse_embed, cots, projs):
    batch, width, _ = sparse_embed.shape
    inputs = [
        pltpu.with_memory_space_constraint(array, pltpu.HBM)
        for array in (assignment, sparse_embed, *cots, *projs)
    ]
    return pl.pallas_call(
        pack_kernel,
        out_shape=jax.ShapeDtypeStruct((batch // 2, width, PACKED), BF16),
        in_specs=[pl.BlockSpec(memory_space=pltpu.SMEM)]
        + [pl.BlockSpec(memory_space=pltpu.HBM)] * len(inputs),
        out_specs=pl.BlockSpec(memory_space=pltpu.VMEM),
        scratch_shapes=[pltpu.VMEM((batch, 128), F32)]
        + [pltpu.VMEM(array.shape, array.dtype) for array in inputs]
        + [pltpu.SemaphoreType.DMA((len(inputs),))],
        compiler_params=pltpu.CompilerParams(vmem_limit_bytes=32 * 2**20),
        name="pack_rows",
    )(assignment, *inputs)


def state_kernel(factor, packed_ref, interest_ref, sent_ref):
    contract_rows = (((0,), (0,)), ((), ()))
    contract_lanes = (((1,), (1,)), ((), ()))
    side = packed_ref[:, SIDE:]
    proj = side[:, 2 * STATE : 3 * STATE]
    total_int, total_spa = None, None
    for slot in range(2):
        interest = interest_ref[slot]
        sparse = packed_ref[:, slot * EMB : (slot + 1) * EMB]
        cot = side[:, slot * STATE : (slot + 1) * STATE]
        left_int = jnp.concatenate([proj[:, :RANK], cot[:, :RANK]], axis=1)
        left_spa = jnp.concatenate([proj[:, RANK:], cot[:, RANK:]], axis=1)
        summed = lax.dot_general(
            left_int, interest, contract_rows, preferred_element_type=F32
        ) + lax.dot_general(left_spa, sparse, contract_rows, preferred_element_type=F32)
        is_state = lax.broadcasted_iota(jnp.int32, summed.shape, 0) < RANK
        rounded = jnp.where(is_state, summed, summed * factor).astype(BF16)
        sent_ref[slot] = rounded
        grad = rounded[RANK:, :]
        part_int = lax.dot_general(grad, interest, contract_lanes, preferred_element_type=F32)
        part_spa = lax.dot_general(grad, sparse, contract_lanes, preferred_element_type=F32)
        total_int = part_int if total_int is None else total_int + part_int
        total_spa = part_spa if total_spa is None else total_spa + part_spa
    sent_ref[2] = jnp.concatenate([total_int, total_spa], axis=0).astype(BF16)


def make_state(packed, interest):
    vmem = pl.BlockSpec(memory_space=pltpu.VMEM)
    return pl.pallas_call(
        functools.partial(state_kernel, 1.0 / math.sqrt(EMB)),
        out_shape=jax.ShapeDtypeStruct((3, STATE, EMB), BF16),
        in_specs=[vmem, vmem],
        out_specs=vmem,
        compiler_params=pltpu.CompilerParams(vmem_limit_bytes=32 * 2**20),
        name="make_state",
    )(packed, interest)


def columns_kernel(factor, wanted_ref, cot_int_ref, cot_spa_ref, proj_int_ref, proj_spa_ref, out_ref, rows):
    users, width = wanted_ref.shape[1], proj_int_ref.shape[0]
    row_of = lax.broadcasted_iota(jnp.int32, (users, users), 0)
    pick = (row_of == wanted_ref[...]).astype(BF16)
    for kind, (cot_ref, proj_ref) in enumerate(
        ((cot_int_ref, proj_int_ref), (cot_spa_ref, proj_spa_ref))
    ):
        for j in range(width):
            cot = lax.dot_general(
                pick, cot_ref[:, j, :], (((0,), (1,)), ((), ())), preferred_element_type=F32
            )
            proj = jnp.broadcast_to(proj_ref[j : j + 1, :].astype(F32), (users, RANK))
            row = [cot * factor, proj, jnp.zeros((users, 128 - STATE), F32)]
            rows[pl.ds(kind * width + j, users, stride=8), :] = jnp.concatenate(row, axis=1)
    height = out_ref.shape[2]
    for member in range(out_ref.shape[0]):
        turned = jnp.transpose(rows[member * height : (member + 1) * height, :])
        out_ref[member] = turned[:STATE, :].astype(BF16)


def left_columns(wanted, cots, projs, factor):
    vmem = pl.BlockSpec(memory_space=pltpu.VMEM)
    users = wanted.shape[1]
    return pl.pallas_call(
        functools.partial(columns_kernel, factor),
        out_shape=jax.ShapeDtypeStruct((MEMBERS, STATE, users * 8 // MEMBERS), BF16),
        in_specs=[vmem] * 5,
        out_specs=vmem,
        scratch_shapes=[pltpu.VMEM((users * 8, 128), F32)],
        compiler_params=pltpu.CompilerParams(vmem_limit_bytes=32 * 2**20),
        name="left_columns",
    )(wanted, *cots, *projs)


def left_kernel(*refs):
    columns, left_ref = refs[:-1], refs[-1]
    blocks, height, depth = left_ref.shape[1:]
    same = lax.broadcasted_iota(jnp.int32, (STATE, STATE), 0) == lax.broadcasted_iota(
        jnp.int32, (STATE, STATE), 1
    )
    repeat = jnp.concatenate([same.astype(BF16)] * (depth // STATE), axis=1)
    owner = lax.broadcasted_iota(jnp.int32, (height, STATE), 0) // 8
    mask = jnp.concatenate([(owner == i).astype(F32) for i in range(depth // STATE)], axis=1)
    for member, column_ref in enumerate(columns):
        wide = lax.dot_general(
            column_ref[...], repeat, (((0,), (0,)), ((), ())), preferred_element_type=F32
        )
        for block in range(blocks):
            part = wide[block * height : (block + 1) * height, :]
            left_ref[member, block] = (part * mask).astype(BF16)


def left_blocks(columns):
    vmem = pl.BlockSpec(memory_space=pltpu.VMEM)
    per_block = 2 * NEAR
    height = per_block * 8
    blocks = columns[0].shape[1] // height
    return pl.pallas_call(
        left_kernel,
        out_shape=jax.ShapeDtypeStruct((len(columns), blocks, height, per_block * STATE), BF16),
        in_specs=[vmem] * len(columns),
        out_specs=vmem,
        compiler_params=pltpu.CompilerParams(vmem_limit_bytes=32 * 2**20),
        name="left_blocks",
    )(*columns)


def embed_kernel(shards, place_ref, left_ref, got_ref, *refs):
    outs, spread_ref, states = refs[:MEMBERS], refs[MEMBERS], refs[MEMBERS + 1]
    total = None
    for source in range(states.shape[0]):
        for slot in range(2):
            states[source, slot * STATE : (slot + 1) * STATE, :] = got_ref[3 * source + slot]
        part = got_ref[3 * source + 2].astype(F32)
        total = part if total is None else total + part
    total = jnp.concatenate([total, jnp.zeros((128 - STATE, total.shape[1]), F32)], axis=0)
    width = spread_ref.shape[1]
    halves = 2
    columns = total.shape[1] // halves
    for half in range(halves):
        mine = pltpu.roll(
            total[:, half * columns : (half + 1) * columns],
            columns - place_ref[0] * PAIR * width,
            1,
        )
        turned = jnp.transpose(mine)
        for member in range(PAIR):
            row = turned[member * width : (member + 1) * width, :]
            for shard in range(shards):
                spread_ref[(half * shards + shard) * PAIR + member] = row
    for block in range(left_ref.shape[1]):
        right = states[block * NEAR : (block + 1) * NEAR].reshape(NEAR * 2 * STATE, EMB)
        for member, out_ref in enumerate(outs):
            got = jnp.dot(left_ref[member, block], right, preferred_element_type=F32)
            for i in range(2 * NEAR):
                for kind in range(2):
                    first = 8 * i + kind * width
                    out_ref[block * 2 * NEAR + i, kind] = got[first : first + width, :].astype(BF16)


def embed_rows(place, left, gathered, shards, width):
    vmem = pl.BlockSpec(memory_space=pltpu.VMEM)
    sources, emb = gathered.shape[0] // 3, gathered.shape[2]
    out = jax.ShapeDtypeStruct((2 * sources, 2, width, emb), BF16)
    return pl.pallas_call(
        functools.partial(embed_kernel, shards),
        out_shape=(out,) * MEMBERS
        + (jax.ShapeDtypeStruct((2 * shards * PAIR, width, 128), F32),),
        in_specs=[pl.BlockSpec(memory_space=pltpu.SMEM), vmem, vmem],
        out_specs=(vmem,) * (MEMBERS + 1),
        scratch_shapes=[pltpu.VMEM((sources, 2 * STATE, emb), BF16)],
        compiler_params=pltpu.CompilerParams(vmem_limit_bytes=32 * 2**20),
        name="embed_rows",
    )(place, left, gathered)


def scatter_kernel(rows_ref, *refs):
    sources, (int_ref, spa_ref) = refs[:-2], refs[-2:]
    for member, source in enumerate(sources):
        users = source.shape[0]
        for user in range(users):
            row = rows_ref[member * users + user]
            int_ref[row] = source[user, 0]
            spa_ref[row] = source[user, 1]


def scatter_rows(rows, sources, width):
    vmem = pl.BlockSpec(memory_space=pltpu.VMEM)
    out = jax.ShapeDtypeStruct((rows.shape[0], width, EMB), BF16)
    return pl.pallas_call(
        scatter_kernel,
        out_shape=(out, out),
        in_specs=[pl.BlockSpec(memory_space=pltpu.SMEM)] + [vmem] * len(sources),
        out_specs=(vmem, vmem),
        compiler_params=pltpu.CompilerParams(vmem_limit_bytes=32 * 2**20),
        name="scatter_rows",
    )(rows, *sources)


def on_device(
    history,
    queries,
    lengths,
    assignment,
    key_weight,
    key_gain,
    interest_gain,
    sparse_embed,
    proj_interest,
    proj_sparse,
    cot_interest,
    cot_sparse,
):
    batch_rows = assignment[0]
    batch_local, width, _ = sparse_embed.shape
    devices = batch_local // 2
    tensor = lax.axis_size("tensor")
    halves = lax.axis_size("half")
    factor = 1.0 / math.sqrt(EMB)

    cots = [cot_interest.transpose(2, 1, 0), cot_sparse.transpose(2, 1, 0)]
    packed = pack(assignment, sparse_embed, cots, [proj_interest, proj_sparse])
    arrived = lax.all_to_all(packed, ALL, split_axis=0, concat_axis=0, tiled=True)

    interest = encode_users(history, queries, lengths, key_weight, key_gain, interest_gain)

    far_count = tensor // PAIR
    far_groups = [[i + PAIR * m for m in range(far_count)] for i in range(PAIR)]
    my_half = lax.axis_index("half")
    my_tensor = lax.axis_index("tensor")
    tables = batch_rows.reshape(halves, far_count, PAIR, 2).transpose(0, 2, 1, 3)
    tables = jnp.where(my_half == 0, tables, tables[::-1])
    tables = jnp.where(my_tensor % PAIR == 0, tables, tables[:, ::-1])
    ordered_rows = tables.reshape(batch_local)
    flips = [
        [(h * tensor + z, (h ^ over_half) * tensor + (z ^ over_pair)) for h in range(halves) for z in range(tensor)]
        for over_half in range(halves)
        for over_pair in range(PAIR)
    ]
    wanted, interest = lax.optimization_barrier((ordered_rows[None], interest))
    columns = left_columns(wanted, cots, [proj_interest, proj_sparse], factor)
    left = left_blocks(
        [columns[0]] + [lax.ppermute(columns[i], ALL, flips[i]) for i in range(1, MEMBERS)]
    )
    interest, left = lax.optimization_barrier((interest, left))

    sent = make_state(arrived.reshape(devices * width, PACKED), interest)
    gathered = lax.all_gather(sent, "tensor", axis=0, tiled=True, axis_index_groups=far_groups)

    shards = lax.axis_size("dp")
    pair = my_tensor // PAIR
    *outs, spread = embed_rows(
        pair.reshape(1).astype(jnp.int32), left, gathered, shards, width
    )
    sum_groups = [
        [
            (half * shards + shard) * tensor + PAIR * m + i
            for half in range(halves)
            for shard in range(shards)
            for i in range(PAIR)
        ]
        for m in range(far_count)
    ]
    shares = lax.all_to_all(
        spread,
        ("half", "dp", "tensor"),
        split_axis=0,
        concat_axis=0,
        tiled=True,
        axis_index_groups=sum_groups,
    )
    batch_total = shards * batch_local
    proj_grads = jnp.sum(shares, axis=0)[:, :STATE] / batch_total

    sent_order = [3, 1, 2]
    sources = [outs[0]] + [lax.ppermute(outs[i], ALL, flips[i]) for i in sent_order]
    by_member = ordered_rows.reshape(MEMBERS, batch_local // MEMBERS)
    sent_rows = jnp.stack([by_member[i] for i in [0] + sent_order]).reshape(batch_local)
    grad_interest, grad_sparse = scatter_rows(sent_rows, sources, width)
    return (grad_interest, grad_sparse, proj_grads[:, :RANK], proj_grads[:, RANK:])


def solution(mesh):
    placed = (
        P("dp", ("half", "tensor"), None, None),
        P("dp", ("half", "tensor"), None, None),
        P("dp", ("half", "tensor")),
        P("dp", None),
        P(),
        P(),
        P(),
        P("dp", ("half", "tensor"), None),
        P(("half", "tensor"), None),
        P(("half", "tensor"), None),
        P("dp", ("half", "tensor"), None),
        P("dp", ("half", "tensor"), None),
    )
    return jax.shard_map(
        on_device,
        mesh=mesh,
        in_specs=placed,
        out_specs=(
            P("dp", ("half", "tensor"), None),
            P("dp", ("half", "tensor"), None),
            P(("half", "tensor"), None),
            P(("half", "tensor"), None),
        ),
        check_vma=False,
    )
```
